32 devices in a mesh: grp: 2 (over y), gx: 16 (over z, x, core).
Axes of the slice: x: 2, y: 2, z: 4, core: 2. Of those that a mesh axis runs over, the one named last changes fastest.
Arguments:
- adj_final: float32 [16, 16, 64, 256], P('gx', 'grp'), parts along dimension 1, may hold values from -6 to 6
- wind_east: float32 [16, 16, 64, 256], P('gx', 'grp'), parts along dimension 1, may hold values from -0.6 to 0.6
- wind_north: float32 [16, 16, 64, 256], P('gx', 'grp'), parts along dimension 1, may hold values from -0.6 to 0.6
- relax_weight: float32 [4, 8], replicated, may hold values from 0.1 to 0.9
- rim_slot: int32 [21760], P('gx'), may hold values from 0 to 1359, as said below
Outputs:
- adj_initial: float32 [16, 16, 64, 256], P('gx', 'grp'), parts along dimension 1
- adj_rim_start: float32 [16, 21760], P('grp', 'gx'), parts along dimension 0
- adj_rim_end: float32 [16, 21760], P('grp', 'gx'), parts along dimension 0
The draws below stay inside these ranges and needn't reach their ends.
There are 2 independent parts, one for each index of `grp`. The reference program is written for one: setup_inputs(seed, part) draws one part's arguments, and reference() takes and returns one part's arrays. A program takes and returns all parts, laid end to end along the dimension named above; an argument that names none is the same for every part. Nothing has to cross between parts.
Inputs may be any that keep to these rules, and one draw needn't show every extreme that they name: `rim_slot`: each aligned block of 1360 entries holds every number 0 to 1359 once.
All inputs are finite; a program needn't handle non-finite values.
Results may differ from the reference program's by a relative error of at most 0.00002.
Values sent between devices are 32-bit elements; how exact they have to be, the bound alone decides.
A program may use at most 64 MiB of HBM per device.

```python
import jax
import jax.numpy as jnp

TILE_R = 64
TILE_C = 256
COL_TILES = 8
LEVELS = 8
STEPS = 2
ZONE = 5
ROW_TILES = 2
NROW = 128
NCOL = 2048
ROW_BLK = 8
COL_BLK = 128
RIM_BLK = 1360
RIM = 21760
N_GX = 16


def draw_rim_slot(key, part):
    key = jax.random.fold_in(key, 7)
    blocks = RIM // RIM_BLK
    keys = jax.random.split(key, blocks)
    orders = jax.vmap(lambda one_key: jax.random.permutation(one_key, RIM_BLK))(keys)
    return orders.reshape(RIM).astype(jnp.int32)


def level_of(stream_key, shape, shards, smallest, largest):
    gain = 1.0
    for dim, blocks in shards:
        heights = jax.random.uniform(jax.random.fold_in(jax.random.fold_in(stream_key, 6), dim), (blocks,), jnp.float32, smallest / len(shards), largest / len(shards))
        gain = gain * jnp.repeat(jnp.exp(heights), shape[dim] // blocks).reshape((-1,) + (1,) * (len(shape) - 1 - dim))
    return gain


def centred(key, shape, scale, limit, cuts=(), kind=jnp.bfloat16):
    array = scale * jax.random.normal(key, shape, jnp.float32)
    if cuts:
        array = array * level_of(key, shape, cuts, -0.22, 0.18)
    return jnp.clip(array, -limit, limit).astype(kind)


def setup_inputs(seed: int = 0, part: int = 0) -> dict:
    key_list = jax.random.split(jax.random.key(seed), 6)
    own_keys = jax.random.split(jax.random.fold_in(key_list[5], part), 6)
    return {
        "adj_final": centred(own_keys[0], (N_GX, LEVELS, TILE_R, TILE_C), 1.0, 6.0, ((0, 16),), jnp.float32),
        "wind_east": jnp.clip(jax.random.uniform(own_keys[1], (N_GX, LEVELS, TILE_R, TILE_C), jnp.float32, -0.6, 0.6) * level_of(own_keys[1], (N_GX, LEVELS, TILE_R, TILE_C), ((0, 16),), -0.4, 0.0), -0.6, 0.6),
        "wind_north": jnp.clip(jax.random.uniform(own_keys[2], (N_GX, LEVELS, TILE_R, TILE_C), jnp.float32, -0.6, 0.6) * level_of(own_keys[2], (N_GX, LEVELS, TILE_R, TILE_C), ((0, 16),), -0.4, 0.0), -0.6, 0.6),
        "relax_weight": jnp.clip(jax.random.uniform(key_list[3], (ZONE - 1, LEVELS), jnp.float32, 0.1, 0.9), 0.1, 0.9),
        "rim_slot": draw_rim_slot(jax.random.fold_in(key_list[5], 71), part),
    }


diffusion = 0.15

def to_grid(tiles):
    return tiles.reshape(ROW_TILES, COL_TILES, LEVELS, TILE_R, TILE_C).transpose(2, 0, 3, 1, 4).reshape(LEVELS, NROW, NCOL)

def to_tiles(grid):
    return grid.reshape(LEVELS, ROW_TILES, TILE_R, COL_TILES, TILE_C).transpose(1, 3, 0, 2, 4).reshape(N_GX, LEVELS, TILE_R, TILE_C)

def advance(field, wind_east, wind_north):
    padded = jnp.pad(field, ((0, 0), (1, 1), (1, 1)))
    east = padded[:, 1:-1, 2:]
    west = padded[:, 1:-1, :-2]
    north = padded[:, 2:, 1:-1]
    south = padded[:, :-2, 1:-1]
    return (1.0 - 4.0 * diffusion) * field + diffusion * (east + west + north + south) - 0.5 * wind_east * (east - west) - 0.5 * wind_north * (north - south)

def zone_masks(row_total, col_total, relax_weight):
    row_index = jnp.arange(row_total, dtype=jnp.int32)
    column_index = jnp.arange(col_total, dtype=jnp.int32)
    row_distance = jnp.minimum(row_index, row_total - 1 - row_index)
    col_distance = jnp.minimum(column_index, col_total - 1 - column_index)
    distance = jnp.minimum(row_distance[:, None], col_distance[None, :])
    weight = jnp.where(distance == 0, 1.0, 0.0).astype(jnp.float32)[None]
    for cycle in range(1, ZONE):
        inside = jnp.where(distance == cycle, 1.0, 0.0).astype(jnp.float32)[None]
        weight = weight + inside * relax_weight[cycle - 1][:, None, None]
    count = (row_distance < ZONE).astype(jnp.float32)[:, None] + (col_distance < ZONE).astype(jnp.float32)[None, :]
    count = jnp.maximum(count, 1.0)
    return (weight, count)

def boundary_field(rim, rim_slot, count):
    levels = rim.shape[0]
    base = jnp.arange(RIM, dtype=jnp.int32) // RIM_BLK * RIM_BLK
    points = jnp.zeros((levels, RIM), jnp.float32).at[:, base + rim_slot].set(rim)
    points = points.reshape(levels, N_GX, RIM_BLK)
    south_span = ZONE * COL_BLK
    side_span = ZONE * ROW_BLK
    south = points[:, :, :south_span].reshape(levels, N_GX, ZONE, COL_BLK).transpose(0, 2, 1, 3).reshape(levels, ZONE, NCOL)
    north = points[:, :, south_span:2 * south_span].reshape(levels, N_GX, ZONE, COL_BLK).transpose(0, 2, 1, 3).reshape(levels, ZONE, NCOL)
    west = points[:, :, 2 * south_span:2 * south_span + side_span].reshape(levels, N_GX, ZONE, ROW_BLK).transpose(0, 2, 1, 3).reshape(levels, ZONE, NROW)
    east = points[:, :, 2 * south_span + side_span:].reshape(levels, N_GX, ZONE, ROW_BLK).transpose(0, 2, 1, 3).reshape(levels, ZONE, NROW)
    field = jnp.zeros((levels, NROW, NCOL), jnp.float32)
    field = field.at[:, :ZONE, :].add(south)
    field = field.at[:, NROW - ZONE:, :].add(north[:, ::-1, :])
    field = field.at[:, :, :ZONE].add(jnp.transpose(west, (0, 2, 1)))
    field = field.at[:, :, NCOL - ZONE:].add(jnp.transpose(east, (0, 2, 1))[:, :, ::-1])
    return field / count

def reference(adj_final, wind_east, wind_north, relax_weight, rim_slot):
    weight, count = zone_masks(NROW, NCOL, relax_weight)
    east_grid = to_grid(wind_east)
    north_grid = to_grid(wind_north)

    def forward(start, rim_start, rim_end):
        first = boundary_field(rim_start, rim_slot, count)
        last = boundary_field(rim_end, rim_slot, count)
        state = start
        for step in range(1, STEPS + 1):
            fraction = step / (STEPS + 1.0)
            target = (1.0 - fraction) * first + fraction * last
            state = (1.0 - weight) * advance(state, east_grid, north_grid) + weight * target
        return state
    zeros_state = jnp.zeros((LEVELS, NROW, NCOL), jnp.float32)
    zeros_rim = jnp.zeros((LEVELS, RIM), jnp.float32)
    unused_out, pullback = jax.vjp(forward, zeros_state, zeros_rim, zeros_rim)
    adj_start, adj_first, adj_last = pullback(to_grid(adj_final))
    return (to_tiles(adj_start), adj_first, adj_last)
```

```python
import functools

import jax
import jax.numpy as jnp
from jax import lax
from jax.experimental import pallas as pl
from jax.experimental.pallas import tpu as pltpu
from jax.sharding import PartitionSpec as P

COL_TILES = 8
STEPS = 2
ZONE = 5
LANES = 128

diffusion = 0.15


def iota(shape, axis):
    return lax.broadcasted_iota(jnp.int32, shape, axis)


def adjoint_kernel(tile_rows, cb, z_hbm, e_hbm, n_hbm, relax, out, pts,
                   z, e, n, omw, z1, send_col, recv_col, send_row, recv_row,
                   strip, row_out, col_out, row_in, col_in,
                   in_sem, hs_sem, hr_sem, rs_sem, rr_sem, cs_sem, cr_sem):
    levels, tile_r, tile_c = z.shape
    row_blk = tile_r // COL_TILES
    me = lax.axis_index("gx")
    ti = lax.div(me, COL_TILES)
    tj = lax.rem(me, COL_TILES)
    south, north = ti == 0, ti == tile_rows - 1
    west, east = tj == 0, tj == COL_TILES - 1

    loads = [pltpu.make_async_copy(src.at[0], dst, in_sem.at[k])
             for k, (src, dst) in enumerate([(z_hbm, z), (e_hbm, e), (n_hbm, n)])]
    for load in loads:
        load.start()

    ways = [
        (~east, me + 1, ~west, me - 1),
        (~west, me - 1, ~east, me + 1),
        (~north, me + COL_TILES, ~south, me - COL_TILES),
        (~south, me - COL_TILES, ~north, me + COL_TILES),
    ]
    row_source = [lax.div(me, tile_rows), (tile_rows - 1) * COL_TILES + lax.div(me, tile_rows)]
    col_source = [ti * COL_TILES, ti * COL_TILES + COL_TILES - 1]

    barrier = pltpu.get_barrier_semaphore()

    def greet(cond, who):
        @pl.when(cond)
        def _():
            pl.semaphore_signal(barrier, inc=1, device_id={"gx": who},
                                device_id_type=pl.DeviceIdType.MESH)

    for sends, target, receives, source in ways:
        greet(receives, source)
    for source in row_source + col_source:
        greet(source != me, source)

    for d in range(2):
        @pl.when(~ways[d][2])
        def _(d=d):
            for step in range(STEPS):
                recv_col[step, d] = jnp.zeros((tile_r, LANES), jnp.float32)

        @pl.when(~ways[2 + d][2])
        def _(d=d):
            for step in range(STEPS):
                recv_row[step, d] = jnp.zeros((levels, tile_c), jnp.float32)

    row_total, col_total = tile_r * tile_rows, tile_c * COL_TILES
    rows = ti * tile_r + iota((tile_r, tile_c), 0)
    cols = tj * tile_c + iota((tile_r, tile_c), 1)
    distance = jnp.minimum(jnp.minimum(rows, row_total - 1 - rows),
                           jnp.minimum(cols, col_total - 1 - cols))
    for l in range(levels):
        value = jnp.where(distance == 0, 0.0, 1.0)
        for cycle in range(1, ZONE):
            value = jnp.where(distance == cycle, 1.0 - relax[cycle - 1, l], value)
        omw[l] = value

    row_sends = jnp.where(south | north, tile_rows, 0)
    col_sends = jnp.where(west | east, COL_TILES, 0)
    total = row_sends + col_sends
    for sends, _, _, _ in ways:
        total = total + jnp.where(sends, 1, 0)
    row_base, col_base = tj * tile_rows, ti * COL_TILES
    own_row = (south | north) & (me >= row_base) & (me < row_base + tile_rows)
    own_col = west | east
    total = total - jnp.where(own_row, 1, 0) - jnp.where(own_col, 1, 0)

    for load in loads:
        load.wait()
    pl.semaphore_wait(barrier, total)

    lane = iota((tile_r, LANES), 1)
    lane_w = iota((tile_r, tile_c), 1)
    row_w = iota((tile_r, tile_c), 0)

    def halo(step, d):
        sends, target, receives, source = ways[d]
        if d < 2:
            src, dst = send_col.at[step, d], recv_col.at[step, d]
        else:
            src, dst = send_row.at[step, d - 2], recv_row.at[step, d - 2]
        return pltpu.make_async_remote_copy(
            src_ref=src, dst_ref=dst, send_sem=hs_sem.at[step, d], recv_sem=hr_sem.at[step, d],
            device_id={"gx": jnp.where(sends, target, source)},
            device_id_type=pl.DeviceIdType.MESH)

    def apply(source, dest, step):
        packs = [jnp.zeros((tile_r, LANES), jnp.float32)] * 2
        for l in range(levels):
            y = omw[l] * source[l]
            ew, nw = 0.5 * e[l], 0.5 * n[l]
            dy = diffusion * y
            ey, ny = ew * y, nw * y
            pushed = pltpu.roll(dy - ey, 1, 1)
            pulled = pltpu.roll(dy + ey, tile_c - 1, 1)
            northward, southward = dy - ny, dy + ny
            send_row[step, 0, l:l + 1, :] = northward[tile_r - 1:tile_r]
            send_row[step, 1, l:l + 1, :] = southward[0:1]
            up = pltpu.roll(northward, 1, 0)
            down = pltpu.roll(southward, tile_r - 1, 0)
            first, last = pushed[:, :LANES], pulled[:, tile_c - LANES:]
            packs[0] = jnp.where(lane == l, pltpu.roll(first, l, 1) if l else first, packs[0])
            packs[1] = jnp.where(lane == l, pltpu.roll(last, l + 1, 1), packs[1])
            dest[l] = ((1.0 - 4.0 * diffusion) * y
                       + jnp.where(lane_w == 0, 0.0, pushed)
                       + jnp.where(lane_w == tile_c - 1, 0.0, pulled)
                       + jnp.where(row_w == 0, 0.0, up)
                       + jnp.where(row_w == tile_r - 1, 0.0, down))
        for d in range(2):
            send_col[step, d] = packs[d]
        for d in range(4):
            @pl.when(ways[d][0])
            def _(d=d):
                halo(step, d).start()

    def finish(dest, step):
        for d in range(4):
            @pl.when(ways[d][2])
            def _(d=d):
                halo(step, d).wait_recv()
        left, right = recv_col[step, 0], recv_col[step, 1]
        for l in range(levels):
            moved = pltpu.roll(left, LANES - l, 1) if l else left
            dest[l, :, :LANES] = dest[l, :, :LANES] + jnp.where(lane == 0, moved, 0.0)
            moved = pltpu.roll(right, LANES - 1 - l, 1)
            dest[l, :, tile_c - LANES:] = dest[l, :, tile_c - LANES:] + jnp.where(
                lane == LANES - 1, moved, 0.0)
            dest[l, 0:1, :] = dest[l, 0:1, :] + recv_row[step, 0, l:l + 1, :]
            dest[l, tile_r - 1:tile_r, :] = (
                dest[l, tile_r - 1:tile_r, :] + recv_row[step, 1, l:l + 1, :])

    apply(z, z1, 0)
    finish(z1, 0)

    def two(t2, t1):
        one, third = 2.0 / (STEPS + 1.0), 1.0 / (STEPS + 1.0)
        return (1.0 - one) * t2 + (1.0 - third) * t1, one * t2 + third * t1

    lane_p = iota((2 * levels, LANES), 1)
    lane_l = iota((levels, LANES), 1)

    def piece(out_ref, in_ref, k, slot, s_sem, r_sem, target):
        return pltpu.make_async_remote_copy(
            src_ref=out_ref.at[k], dst_ref=in_ref.at[slot], send_sem=s_sem.at[k],
            recv_sem=r_sem.at[slot], device_id={"gx": target},
            device_id_type=pl.DeviceIdType.MESH)

    def each_piece(out_ref, in_ref, count, base, slots, s_sem, r_sem, start):
        for slot, cond in enumerate(slots):
            for k in range(count):
                target = base + k

                @pl.when(cond & (target != me))
                def _():
                    copy = piece(out_ref, in_ref, k, slot, s_sem, r_sem, target)
                    if start:
                        copy.start()
                    else:
                        copy.wait_send()

                if start:
                    @pl.when(cond & (target == me))
                    def _():
                        in_ref[slot] = out_ref[k]

    row_args = (row_out, row_in, tile_rows, row_base, (south, north), rs_sem, rr_sem)
    col_args = (col_out, col_in, COL_TILES, col_base, (west, east), cs_sem, cr_sem)

    @pl.when(south | north)
    def _():
        col_index = tj * tile_c + iota((levels, tile_c), 1)
        inverse = jnp.where(jnp.minimum(col_index, col_total - 1 - col_index) < ZONE, 0.5, 1.0)
        for w in range(ZONE):
            def pick(ref):
                return jnp.where(north, ref[:, tile_r - 1 - w, :], ref[:, w, :])
            weight = (1.0 - pick(omw)) * inverse
            values = jnp.concatenate(two(weight * pick(z), weight * pick(z1)), axis=0)
            for t in range(tile_rows):
                if cb % LANES == 0:
                    row_out[t, :, w * cb:(w + 1) * cb] = values[:, t * cb:(t + 1) * cb]
                    continue
                block, offset = divmod(w * cb, LANES)
                from_block, from_offset = divmod(t * cb, LANES)
                shift = (offset - from_offset) % LANES
                part = values[:, from_block * LANES:(from_block + 1) * LANES]
                part = pltpu.roll(part, shift, 1) if shift else part
                there = slice(block * LANES, (block + 1) * LANES)
                if offset:
                    part = jnp.where(lane_p >= offset, part, row_out[t, :, there])
                row_out[t, :, there] = part
        each_piece(*row_args, True)

    @pl.when(west | east)
    def _():
        row_index = ti * tile_r + iota((tile_r, LANES), 0)
        inverse = jnp.where(jnp.minimum(row_index, row_total - 1 - row_index) < ZONE, 0.5, 1.0)
        for l in range(levels):
            def pick(ref):
                return jnp.where(east, ref[l, :, tile_c - LANES:], ref[l, :, :LANES])
            weight = (1.0 - pick(omw)) * inverse
            values = jnp.concatenate(two(weight * pick(z), weight * pick(z1)), axis=0)
            turned = jnp.transpose(values)
            strip[:, l, :] = jnp.where(east, turned[LANES - 8:], turned[:8])
        lines = [jnp.where(east, strip[7 - w], strip[w]) for w in range(ZONE)]
        for k in range(COL_TILES):
            for f in range(2):
                value = jnp.zeros((levels, LANES), jnp.float32)
                for w in range(ZONE):
                    shift = (w * row_blk - f * tile_r - k * row_blk) % LANES
                    moved = pltpu.roll(lines[w], shift, 1) if shift else lines[w]
                    inside = (lane_l >= w * row_blk) & (lane_l < (w + 1) * row_blk)
                    value = jnp.where(inside, moved, value)
                col_out[k, f * levels:(f + 1) * levels, :] = value
        each_piece(*col_args, True)

    apply(z1, out, 1)
    finish(out, 1)

    for slot in range(2):
        @pl.when(row_source[slot] != me)
        def _(slot=slot):
            piece(row_out, row_in, 0, slot, rs_sem, rr_sem, row_source[slot]).wait_recv()

        @pl.when(col_source[slot] != me)
        def _(slot=slot):
            piece(col_out, col_in, 0, slot, cs_sem, cr_sem, col_source[slot]).wait_recv()

    width = row_in.shape[2]
    side = ZONE * row_blk
    pts[:, :width] = row_in[0]
    pts[:, width:2 * width] = row_in[1]
    pts[:, 2 * width:] = jnp.where(lane_p < side, col_in[0], pltpu.roll(col_in[1], side, 1))

    for step in range(STEPS):
        for d in range(4):
            @pl.when(ways[d][0])
            def _(step=step, d=d):
                halo(step, d).wait_send()
    each_piece(*row_args, False)
    each_piece(*col_args, False)


def order_kernel(cb, width, pts, slot_ref, first_out, last_out, index):
    levels, rim_blk = first_out.shape
    span = ZONE * cb
    blocks = pts.shape[1] // LANES
    index[...] = jnp.zeros(index.shape, jnp.int32)
    index[:, :rim_blk] = jnp.broadcast_to(slot_ref[...], (2 * levels, rim_blk))
    for s in range(0, rim_blk, LANES):
        q = index[:, s:s + LANES]
        place = jnp.where(q < span, q, jnp.where(q < 2 * span, q + (width - span),
                                                 q + 2 * (width - span)))
        high, low = place // LANES, place % LANES
        total = jnp.zeros((2 * levels, LANES), jnp.float32)
        for b in range(blocks):
            found = jnp.take_along_axis(pts[:, b * LANES:(b + 1) * LANES], low, axis=1)
            total = jnp.where(high == b, found, total)
        size = min(LANES, rim_blk - s)
        first_out[:, s:s + size] = total[:levels, :size]
        last_out[:, s:s + size] = total[levels:, :size]


def body(adj_final, wind_east, wind_north, relax_weight, rim_slot):
    _, levels, tile_r, tile_c = adj_final.shape
    tile_count = lax.axis_size("gx")
    tile_rows = tile_count // COL_TILES
    cb = tile_c // tile_rows
    width = -(-ZONE * cb // LANES) * LANES
    f32 = jnp.float32
    field = pltpu.VMEM((levels, tile_r, tile_c), f32)
    dma = pltpu.SemaphoreType.DMA
    vmem, anywhere = pl.BlockSpec(memory_space=pltpu.VMEM), pl.BlockSpec(memory_space=pl.ANY)
    total = 2 * width + LANES
    adj, pts = pl.pallas_call(
        functools.partial(adjoint_kernel, tile_rows, cb),
        out_shape=(jax.ShapeDtypeStruct((levels, tile_r, tile_c), f32),
                   jax.ShapeDtypeStruct((2 * levels, total), f32)),
        in_specs=[anywhere] * 3 + [pl.BlockSpec(memory_space=pltpu.SMEM)],
        out_specs=(vmem, vmem),
        scratch_shapes=[
            field, field, field, field, field,
            pltpu.VMEM((STEPS, 2, tile_r, LANES), f32),
            pltpu.VMEM((STEPS, 2, tile_r, LANES), f32),
            pltpu.VMEM((STEPS, 2, levels, tile_c), f32),
            pltpu.VMEM((STEPS, 2, levels, tile_c), f32),
            pltpu.VMEM((8, levels, LANES), f32),
            pltpu.VMEM((tile_rows, 2 * levels, width), f32),
            pltpu.VMEM((COL_TILES, 2 * levels, LANES), f32),
            pltpu.VMEM((2, 2 * levels, width), f32),
            pltpu.VMEM((2, 2 * levels, LANES), f32),
            dma((3,)), dma((STEPS, 4)), dma((STEPS, 4)),
            dma((tile_rows,)), dma((2,)), dma((COL_TILES,)), dma((2,)),
        ],
        compiler_params=pltpu.CompilerParams(
            collective_id=0, has_side_effects=True, vmem_limit_bytes=32 * 1024 * 1024),
        cost_estimate=pl.CostEstimate(flops=10_000_000, bytes_accessed=2_200_000,
                                      transcendentals=0),
    )(adj_final, wind_east, wind_north, relax_weight)
    rim_blk = rim_slot.shape[0]
    padded = -(-rim_blk // LANES) * LANES
    first, last = pl.pallas_call(
        functools.partial(order_kernel, cb, width),
        out_shape=(jax.ShapeDtypeStruct((levels, rim_blk), f32),) * 2,
        in_specs=[vmem, vmem],
        out_specs=(vmem, vmem),
        scratch_shapes=[pltpu.VMEM((2 * levels, padded), jnp.int32)],
    )(pts, rim_slot.reshape(1, rim_blk))
    return (adj[None], first, last)


def solution(mesh):
    return jax.shard_map(
        body,
        mesh=mesh,
        in_specs=(
            P("gx", "grp", None, None),
            P("gx", "grp", None, None),
            P("gx", "grp", None, None),
            P(),
            P("gx"),
        ),
        out_specs=(P("gx", "grp", None, None), P("grp", "gx"), P("grp", "gx")),
        check_vma=False,
    )
```

```python
import functools

import jax
import jax.numpy as jnp
from jax import lax
from jax.experimental import pallas as pl
from jax.experimental.pallas import tpu as pltpu
from jax.sharding import PartitionSpec as P

COL_TILES = 8
STEPS = 2
ZONE = 5
LANES = 128

diffusion = 0.15


def iota(shape, axis):
    return lax.broadcasted_iota(jnp.int32, shape, axis)


def adjoint_kernel(tile_rows, cb, z_hbm, e_hbm, n_hbm, relax_hbm, out, pts,
                   relax, z, e, n, omw, z1, send_col, recv_col, send_row, recv_row,
                   early, strip, row_out, col_out, row_in, col_in,
                   relax_sem, in_sem, hs_sem, hr_sem, rs_sem, rr_sem, cs_sem, cr_sem):
    levels, tile_r, tile_c = z.shape
    row_blk = tile_r // COL_TILES
    me = lax.axis_index("gx")
    ti = lax.div(me, COL_TILES)
    tj = lax.rem(me, COL_TILES)
    south, north = ti == 0, ti == tile_rows - 1
    west, east = tj == 0, tj == COL_TILES - 1

    loads = [pltpu.make_async_copy(src.at[0], dst, in_sem.at[k])
             for k, (src, dst) in enumerate([(z_hbm, z), (e_hbm, e), (n_hbm, n)])]
    relax_load = pltpu.make_async_copy(relax_hbm, relax, relax_sem)
    relax_load.start()
    for load in loads:
        load.start()

    ways = [
        (~east, me + 1, ~west, me - 1),
        (~west, me - 1, ~east, me + 1),
        (~north, me + COL_TILES, ~south, me - COL_TILES),
        (~south, me - COL_TILES, ~north, me + COL_TILES),
    ]
    row_source = [lax.div(me, tile_rows), (tile_rows - 1) * COL_TILES + lax.div(me, tile_rows)]
    col_source = [ti * COL_TILES, ti * COL_TILES + COL_TILES - 1]

    barrier = pltpu.get_barrier_semaphore()

    def greet(cond, who):
        @pl.when(cond)
        def _():
            pl.semaphore_signal(barrier, inc=1, device_id={"gx": who},
                                device_id_type=pl.DeviceIdType.MESH)

    for sends, target, receives, source in ways:
        greet(receives, source)
    for source in row_source + col_source:
        greet(source != me, source)

    for d in range(2):
        @pl.when(~ways[d][2])
        def _(d=d):
            for step in range(STEPS):
                recv_col[step, d] = jnp.zeros((tile_r, LANES), jnp.float32)

        @pl.when(~ways[2 + d][2])
        def _(d=d):
            for step in range(STEPS):
                recv_row[step, d] = jnp.zeros((levels, tile_c), jnp.float32)

    row_total, col_total = tile_r * tile_rows, tile_c * COL_TILES
    rows = ti * tile_r + iota((tile_r, tile_c), 0)
    cols = tj * tile_c + iota((tile_r, tile_c), 1)
    distance = jnp.minimum(jnp.minimum(rows, row_total - 1 - rows),
                           jnp.minimum(cols, col_total - 1 - cols))
    relax_load.wait()
    for l in range(levels):
        value = jnp.where(distance == 0, 0.0, 1.0)
        for cycle in range(1, ZONE):
            value = jnp.where(distance == cycle, 1.0 - relax[cycle - 1, l], value)
        omw[l] = value

    row_sends = jnp.where(south | north, tile_rows, 0)
    col_sends = jnp.where(west | east, COL_TILES, 0)
    total = row_sends + col_sends
    for sends, _, _, _ in ways:
        total = total + jnp.where(sends, 1, 0)
    row_base, col_base = tj * tile_rows, ti * COL_TILES
    own_row = (south | north) & (me >= row_base) & (me < row_base + tile_rows)
    own_col = west | east
    total = total - jnp.where(own_row, 1, 0) - jnp.where(own_col, 1, 0)

    for load in loads:
        load.wait()

    lane = iota((tile_r, LANES), 1)
    lane_w = iota((tile_r, tile_c), 1)
    row_w = iota((tile_r, tile_c), 0)

    def halo(step, d):
        sends, target, receives, source = ways[d]
        if d < 2:
            src, dst = send_col.at[step, d], recv_col.at[step, d]
        else:
            src, dst = send_row.at[step, d - 2], recv_row.at[step, d - 2]
        return pltpu.make_async_remote_copy(
            src_ref=src, dst_ref=dst, send_sem=hs_sem.at[step, d], recv_sem=hr_sem.at[step, d],
            device_id={"gx": jnp.where(sends, target, source)},
            device_id_type=pl.DeviceIdType.MESH)

    def edges(source, step):
        def weighted(place):
            return omw[place] * source[place]
        ends = (slice(None), tile_r - 1, slice(None)), (slice(None), 0, slice(None))
        send_row[step, 0] = (diffusion - 0.5 * n[ends[0]]) * weighted(ends[0])
        send_row[step, 1] = (diffusion + 0.5 * n[ends[1]]) * weighted(ends[1])
        packs = [jnp.zeros((tile_r, LANES), jnp.float32)] * 2
        for l in range(levels):
            place = (l, slice(None), slice(tile_c - LANES, tile_c))
            value = (diffusion - 0.5 * e[place]) * weighted(place)
            packs[0] = jnp.where(lane == l, pltpu.roll(value, l + 1, 1), packs[0])
            place = (l, slice(None), slice(0, LANES))
            value = (diffusion + 0.5 * e[place]) * weighted(place)
            packs[1] = jnp.where(lane == l, pltpu.roll(value, l, 1) if l else value, packs[1])
        for d in range(2):
            send_col[step, d] = packs[d]
        if step == 0:
            pl.semaphore_wait(barrier, total)
        for d in range(4):
            @pl.when(ways[d][0])
            def _(d=d):
                halo(step, d).start()

    def interior(source, dest):
        for l in range(levels):
            y = omw[l] * source[l]
            dy = diffusion * y
            ey, ny = 0.5 * e[l] * y, 0.5 * n[l] * y
            pushed = pltpu.roll(dy - ey, 1, 1)
            pulled = pltpu.roll(dy + ey, tile_c - 1, 1)
            up = pltpu.roll(dy - ny, 1, 0)
            down = pltpu.roll(dy + ny, tile_r - 1, 0)
            dest[l] = ((1.0 - 4.0 * diffusion) * y
                       + jnp.where(lane_w == 0, 0.0, pushed)
                       + jnp.where(lane_w == tile_c - 1, 0.0, pulled)
                       + jnp.where(row_w == 0, 0.0, up)
                       + jnp.where(row_w == tile_r - 1, 0.0, down))

    def finish(dest, step):
        for d in range(4):
            @pl.when(ways[d][2])
            def _(d=d):
                halo(step, d).wait_recv()
        left, right = recv_col[step, 0], recv_col[step, 1]
        for l in range(levels):
            moved = pltpu.roll(left, LANES - l, 1) if l else left
            dest[l, :, :LANES] = dest[l, :, :LANES] + jnp.where(lane == 0, moved, 0.0)
            moved = pltpu.roll(right, LANES - 1 - l, 1)
            dest[l, :, tile_c - LANES:] = dest[l, :, tile_c - LANES:] + jnp.where(
                lane == LANES - 1, moved, 0.0)
            dest[l, 0:1, :] = dest[l, 0:1, :] + recv_row[step, 0, l:l + 1, :]
            dest[l, tile_r - 1:tile_r, :] = (
                dest[l, tile_r - 1:tile_r, :] + recv_row[step, 1, l:l + 1, :])

    half = levels // 2

    def turned_columns(ref):
        row_index = ti * tile_r + iota((tile_r, LANES), 0)
        inverse = jnp.where(jnp.minimum(row_index, row_total - 1 - row_index) < ZONE, 0.5, 1.0)
        result = []
        for m in range(half):
            parts = []
            for l in (m, m + half):
                def pick(r, l=l):
                    return jnp.where(east, r[l, :, tile_c - LANES:], r[l, :, :LANES])
                parts.append((1.0 - pick(omw)) * inverse * pick(ref))
            turned = jnp.transpose(jnp.concatenate(parts, axis=0))
            result.append(jnp.where(east, turned[LANES - 8:], turned[:8]))
        return result

    edges(z, 0)
    interior(z, z1)

    @pl.when(west | east)
    def _():
        for m, turned in enumerate(turned_columns(z)):
            early[m] = turned

    finish(z1, 0)
    edges(z1, 1)

    def two(t2, t1):
        one, third = 2.0 / (STEPS + 1.0), 1.0 / (STEPS + 1.0)
        return (1.0 - one) * t2 + (1.0 - third) * t1, one * t2 + third * t1

    lane_p = iota((2 * levels, LANES), 1)
    lane_l = iota((levels, LANES), 1)

    def piece(out_ref, in_ref, k, slot, s_sem, r_sem, target):
        return pltpu.make_async_remote_copy(
            src_ref=out_ref.at[k], dst_ref=in_ref.at[slot], send_sem=s_sem.at[k],
            recv_sem=r_sem.at[slot], device_id={"gx": target},
            device_id_type=pl.DeviceIdType.MESH)

    def each_piece(out_ref, in_ref, count, base, slots, s_sem, r_sem, start):
        for slot, cond in enumerate(slots):
            for k in range(count):
                target = base + k

                @pl.when(cond & (target != me))
                def _():
                    copy = piece(out_ref, in_ref, k, slot, s_sem, r_sem, target)
                    if start:
                        copy.start()
                    else:
                        copy.wait_send()

                if start:
                    @pl.when(cond & (target == me))
                    def _():
                        in_ref[slot] = out_ref[k]

    row_args = (row_out, row_in, tile_rows, row_base, (south, north), rs_sem, rr_sem)
    col_args = (col_out, col_in, COL_TILES, col_base, (west, east), cs_sem, cr_sem)

    @pl.when(south | north)
    def _():
        col_index = tj * tile_c + iota((levels, tile_c), 1)
        inverse = jnp.where(jnp.minimum(col_index, col_total - 1 - col_index) < ZONE, 0.5, 1.0)
        for w in range(ZONE):
            def pick(ref):
                return jnp.where(north, ref[:, tile_r - 1 - w, :], ref[:, w, :])
            weight = (1.0 - pick(omw)) * inverse
            first, last = two(weight * pick(z), weight * pick(z1))
            values = jnp.concatenate([first[:half], last[:half], first[half:], last[half:]], axis=0)
            for t in range(tile_rows):
                if cb % LANES == 0:
                    row_out[t, :, w * cb:(w + 1) * cb] = values[:, t * cb:(t + 1) * cb]
                    continue
                block, offset = divmod(w * cb, LANES)
                from_block, from_offset = divmod(t * cb, LANES)
                shift = (offset - from_offset) % LANES
                part = values[:, from_block * LANES:(from_block + 1) * LANES]
                part = pltpu.roll(part, shift, 1) if shift else part
                there = slice(block * LANES, (block + 1) * LANES)
                if offset:
                    part = jnp.where(lane_p >= offset, part, row_out[t, :, there])
                row_out[t, :, there] = part
        each_piece(*row_args, True)

    @pl.when(west | east)
    def _():
        for m, turned in enumerate(turned_columns(z1)):
            first, last = two(early[m], turned)
            strip[:, m, :] = first
            strip[:, half + m, :] = last
        lines = [jnp.where(east, strip[7 - w], strip[w]) for w in range(ZONE)]
        for k in range(COL_TILES):
            for f in range(2):
                value = jnp.zeros((levels, LANES), jnp.float32)
                for w in range(ZONE):
                    shift = (w * row_blk - f * tile_r - k * row_blk) % LANES
                    moved = pltpu.roll(lines[w], shift, 1) if shift else lines[w]
                    inside = (lane_l >= w * row_blk) & (lane_l < (w + 1) * row_blk)
                    value = jnp.where(inside, moved, value)
                col_out[k, f * levels:(f + 1) * levels, :] = value
        each_piece(*col_args, True)

    interior(z1, out)
    finish(out, 1)

    for slot in range(2):
        @pl.when(row_source[slot] != me)
        def _(slot=slot):
            piece(row_out, row_in, 0, slot, rs_sem, rr_sem, row_source[slot]).wait_recv()

        @pl.when(col_source[slot] != me)
        def _(slot=slot):
            piece(col_out, col_in, 0, slot, cs_sem, cr_sem, col_source[slot]).wait_recv()

    width = row_in.shape[2]
    side = ZONE * row_blk
    pts[:, :width] = row_in[0]
    pts[:, width:2 * width] = row_in[1]
    pts[:, 2 * width:] = jnp.where(lane_p < side, col_in[0], pltpu.roll(col_in[1], side, 1))

    for step in range(STEPS):
        for d in range(4):
            @pl.when(ways[d][0])
            def _(step=step, d=d):
                halo(step, d).wait_send()
    each_piece(*row_args, False)
    each_piece(*col_args, False)


def order_kernel(cb, width, adj, pts, slot_ref, adj_out, first_out, last_out, sem):
    levels, rim_blk = first_out.shape
    half = levels // 2
    span = ZONE * cb
    blocks = pts.shape[1] // LANES
    carry = pltpu.make_async_copy(adj, adj_out.at[0], sem)
    carry.start()
    for s in range(0, rim_blk, LANES):
        size = min(LANES, rim_blk - s)
        q = jnp.broadcast_to(slot_ref[s:s + size].reshape(1, size), (2 * levels, size))
        if size < LANES:
            q = jnp.concatenate([q, jnp.zeros((2 * levels, LANES - size), jnp.int32)], axis=1)
        place = jnp.where(q < span, q, jnp.where(q < 2 * span, q + (width - span),
                                                 q + 2 * (width - span)))
        high, low = place // LANES, place % LANES
        total = jnp.zeros((2 * levels, LANES), jnp.float32)
        for b in range(blocks):
            found = jnp.take_along_axis(pts[:, b * LANES:(b + 1) * LANES], low, axis=1)
            total = jnp.where(high == b, found, total)
        total = total[:, :size]
        first_out[:half, s:s + size] = total[:half]
        last_out[:half, s:s + size] = total[half:levels]
        first_out[half:, s:s + size] = total[levels:levels + half]
        last_out[half:, s:s + size] = total[levels + half:]
    carry.wait()


def body(adj_final, wind_east, wind_north, relax_weight, rim_slot):
    _, levels, tile_r, tile_c = adj_final.shape
    tile_count = lax.axis_size("gx")
    tile_rows = tile_count // COL_TILES
    cb = tile_c // tile_rows
    width = -(-ZONE * cb // LANES) * LANES
    f32 = jnp.float32
    field = pltpu.VMEM((levels, tile_r, tile_c), f32)
    dma = pltpu.SemaphoreType.DMA
    vmem, anywhere = pl.BlockSpec(memory_space=pltpu.VMEM), pl.BlockSpec(memory_space=pl.ANY)
    hbm = pl.BlockSpec(memory_space=pltpu.HBM)
    total = 2 * width + LANES
    adj, pts = pl.pallas_call(
        functools.partial(adjoint_kernel, tile_rows, cb),
        out_shape=(jax.ShapeDtypeStruct((levels, tile_r, tile_c), f32),
                   jax.ShapeDtypeStruct((2 * levels, total), f32)),
        in_specs=[hbm] * 4,
        out_specs=(vmem, vmem),
        scratch_shapes=[
            pltpu.SMEM(relax_weight.shape, f32),
            field, field, field, field, field,
            pltpu.VMEM((STEPS, 2, tile_r, LANES), f32),
            pltpu.VMEM((STEPS, 2, tile_r, LANES), f32),
            pltpu.VMEM((STEPS, 2, levels, tile_c), f32),
            pltpu.VMEM((STEPS, 2, levels, tile_c), f32),
            pltpu.VMEM((levels // 2, 8, LANES), f32),
            pltpu.VMEM((8, levels, LANES), f32),
            pltpu.VMEM((tile_rows, 2 * levels, width), f32),
            pltpu.VMEM((COL_TILES, 2 * levels, LANES), f32),
            pltpu.VMEM((2, 2 * levels, width), f32),
            pltpu.VMEM((2, 2 * levels, LANES), f32),
            dma, dma((3,)), dma((STEPS, 4)), dma((STEPS, 4)),
            dma((tile_rows,)), dma((2,)), dma((COL_TILES,)), dma((2,)),
        ],
        compiler_params=pltpu.CompilerParams(
            collective_id=0, has_side_effects=True),
        cost_estimate=pl.CostEstimate(flops=10_000_000, bytes_accessed=2_200_000,
                                      transcendentals=0),
    )(adj_final, wind_east, wind_north, relax_weight)
    rim = jax.ShapeDtypeStruct((levels, rim_slot.shape[0]), f32)
    return pl.pallas_call(
        functools.partial(order_kernel, cb, width),
        out_shape=(jax.ShapeDtypeStruct((1, levels, tile_r, tile_c), f32), rim, rim),
        in_specs=[anywhere, vmem, vmem],
        out_specs=(hbm, vmem, vmem),
        scratch_shapes=[dma],
        compiler_params=pltpu.CompilerParams(vmem_limit_bytes=8 * 1024 * 1024),
    )(adj, pts, rim_slot)


def solution(mesh):
    return jax.shard_map(
        body,
        mesh=mesh,
        in_specs=(
            P("gx", "grp", None, None),
            P("gx", "grp", None, None),
            P("gx", "grp", None, None),
            P(),
            P("gx"),
        ),
        out_specs=(P("gx", "grp", None, None), P("grp", "gx"), P("grp", "gx")),
        check_vma=False,
    )
```

```python
import functools

import jax
import jax.numpy as jnp
from jax import lax
from jax.experimental import pallas as pl
from jax.experimental.pallas import tpu as pltpu
from jax.sharding import PartitionSpec as P

COL_TILES = 8
STEPS = 2
ZONE = 5
LANES = 128

diffusion = 0.15


def iota(shape, axis):
    return lax.broadcasted_iota(jnp.int32, shape, axis)


def adjoint_kernel(tile_rows, cb, z_hbm, e_hbm, n_hbm, relax_hbm, out, pts,
                   relax, z, e, n, omw, z1, send_col, recv_col, send_row, recv_row,
                   early, strip, row_out, col_out, row_in, col_in,
                   relax_sem, in_sem, hs_sem, hr_sem, rs_sem, rr_sem, cs_sem, cr_sem):
    levels, tile_r, tile_c = z.shape
    row_blk = tile_r // COL_TILES
    me = lax.axis_index("gx")
    ti = lax.div(me, COL_TILES)
    tj = lax.rem(me, COL_TILES)
    south, north = ti == 0, ti == tile_rows - 1
    west, east = tj == 0, tj == COL_TILES - 1

    loads = [pltpu.make_async_copy(src.at[0], dst, in_sem.at[k])
             for k, (src, dst) in enumerate([(z_hbm, z), (e_hbm, e), (n_hbm, n)])]
    relax_load = pltpu.make_async_copy(relax_hbm, relax, relax_sem)
    relax_load.start()
    for load in loads:
        load.start()

    ways = [
        (~east, me + 1, ~west, me - 1),
        (~west, me - 1, ~east, me + 1),
        (~north, me + COL_TILES, ~south, me - COL_TILES),
        (~south, me - COL_TILES, ~north, me + COL_TILES),
    ]
    row_source = [lax.div(me, tile_rows), (tile_rows - 1) * COL_TILES + lax.div(me, tile_rows)]
    col_source = [ti * COL_TILES, ti * COL_TILES + COL_TILES - 1]

    barrier = pltpu.get_barrier_semaphore()

    def greet(cond, who):
        @pl.when(cond)
        def _():
            pl.semaphore_signal(barrier, inc=1, device_id={"gx": who},
                                device_id_type=pl.DeviceIdType.MESH)

    for sends, target, receives, source in ways:
        greet(receives, source)
    for source in row_source + col_source:
        greet(source != me, source)

    for d in range(2):
        @pl.when(~ways[d][2])
        def _(d=d):
            for step in range(STEPS):
                recv_col[step, d] = jnp.zeros((tile_r, LANES), jnp.float32)

        @pl.when(~ways[2 + d][2])
        def _(d=d):
            for step in range(STEPS):
                recv_row[step, d] = jnp.zeros((levels, tile_c), jnp.float32)

    row_total, col_total = tile_r * tile_rows, tile_c * COL_TILES
    rows = ti * tile_r + iota((tile_r, tile_c), 0)
    cols = tj * tile_c + iota((tile_r, tile_c), 1)
    distance = jnp.minimum(jnp.minimum(rows, row_total - 1 - rows),
                           jnp.minimum(cols, col_total - 1 - cols))
    relax_load.wait()
    for l in range(levels):
        value = jnp.where(distance == 0, 0.0, 1.0)
        for cycle in range(1, ZONE):
            value = jnp.where(distance == cycle, 1.0 - relax[cycle - 1, l], value)
        omw[l] = value

    row_sends = jnp.where(south | north, tile_rows, 0)
    col_sends = jnp.where(west | east, COL_TILES, 0)
    total = row_sends + col_sends
    for sends, _, _, _ in ways:
        total = total + jnp.where(sends, 1, 0)
    row_base, col_base = tj * tile_rows, ti * COL_TILES
    own_row = (south | north) & (me >= row_base) & (me < row_base + tile_rows)
    own_col = west | east
    total = total - jnp.where(own_row, 1, 0) - jnp.where(own_col, 1, 0)

    for load in loads:
        load.wait()

    lane = iota((tile_r, LANES), 1)
    lane_w = iota((tile_r, tile_c), 1)
    row_w = iota((tile_r, tile_c), 0)

    def halo(step, d):
        sends, target, receives, source = ways[d]
        if d < 2:
            src, dst = send_col.at[step, d], recv_col.at[step, d]
        else:
            src, dst = send_row.at[step, d - 2], recv_row.at[step, d - 2]
        return pltpu.make_async_remote_copy(
            src_ref=src, dst_ref=dst, send_sem=hs_sem.at[step, d], recv_sem=hr_sem.at[step, d],
            device_id={"gx": jnp.where(sends, target, source)},
            device_id_type=pl.DeviceIdType.MESH)

    def edges(source, step):
        def weighted(place):
            return omw[place] * source[place]
        ends = (slice(None), tile_r - 1, slice(None)), (slice(None), 0, slice(None))
        send_row[step, 0] = (diffusion - 0.5 * n[ends[0]]) * weighted(ends[0])
        send_row[step, 1] = (diffusion + 0.5 * n[ends[1]]) * weighted(ends[1])
        packs = [jnp.zeros((tile_r, LANES), jnp.float32)] * 2
        for l in range(levels):
            place = (l, slice(None), slice(tile_c - LANES, tile_c))
            value = (diffusion - 0.5 * e[place]) * weighted(place)
            packs[0] = jnp.where(lane == l, pltpu.roll(value, l + 1, 1), packs[0])
            place = (l, slice(None), slice(0, LANES))
            value = (diffusion + 0.5 * e[place]) * weighted(place)
            packs[1] = jnp.where(lane == l, pltpu.roll(value, l, 1) if l else value, packs[1])
        for d in range(2):
            send_col[step, d] = packs[d]
        if step == 0:
            pl.semaphore_wait(barrier, total)
        for d in range(4):
            @pl.when(ways[d][0])
            def _(d=d):
                halo(step, d).start()

    def interior(source, dest):
        for l in range(levels):
            y = omw[l] * source[l]
            dy = diffusion * y
            ey, ny = 0.5 * e[l] * y, 0.5 * n[l] * y
            pushed = pltpu.roll(dy - ey, 1, 1)
            pulled = pltpu.roll(dy + ey, tile_c - 1, 1)
            up = pltpu.roll(dy - ny, 1, 0)
            down = pltpu.roll(dy + ny, tile_r - 1, 0)
            dest[l] = ((1.0 - 4.0 * diffusion) * y
                       + jnp.where(lane_w == 0, 0.0, pushed)
                       + jnp.where(lane_w == tile_c - 1, 0.0, pulled)
                       + jnp.where(row_w == 0, 0.0, up)
                       + jnp.where(row_w == tile_r - 1, 0.0, down))

    def finish(dest, step):
        for d in range(4):
            @pl.when(ways[d][2])
            def _(d=d):
                halo(step, d).wait_recv()
        left, right = recv_col[step, 0], recv_col[step, 1]
        for l in range(levels):
            moved = pltpu.roll(left, LANES - l, 1) if l else left
            dest[l, :, :LANES] = dest[l, :, :LANES] + jnp.where(lane == 0, moved, 0.0)
            moved = pltpu.roll(right, LANES - 1 - l, 1)
            dest[l, :, tile_c - LANES:] = dest[l, :, tile_c - LANES:] + jnp.where(
                lane == LANES - 1, moved, 0.0)
            dest[l, 0:1, :] = dest[l, 0:1, :] + recv_row[step, 0, l:l + 1, :]
            dest[l, tile_r - 1:tile_r, :] = (
                dest[l, tile_r - 1:tile_r, :] + recv_row[step, 1, l:l + 1, :])

    half = levels // 2

    def turned_columns(ref):
        row_index = ti * tile_r + iota((tile_r, LANES), 0)
        inverse = jnp.where(jnp.minimum(row_index, row_total - 1 - row_index) < ZONE, 0.5, 1.0)
        result = []
        for m in range(half):
            parts = []
            for l in (m, m + half):
                def pick(r, l=l):
                    return jnp.where(east, r[l, :, tile_c - LANES:], r[l, :, :LANES])
                parts.append((1.0 - pick(omw)) * inverse * pick(ref))
            turned = jnp.transpose(jnp.concatenate(parts, axis=0))
            result.append(jnp.where(east, turned[LANES - 8:], turned[:8]))
        return result

    edges(z, 0)
    interior(z, z1)

    @pl.when(west | east)
    def _():
        for m, turned in enumerate(turned_columns(z)):
            early[m] = turned

    finish(z1, 0)
    edges(z1, 1)

    def two(t2, t1):
        one, third = 2.0 / (STEPS + 1.0), 1.0 / (STEPS + 1.0)
        return (1.0 - one) * t2 + (1.0 - third) * t1, one * t2 + third * t1

    lane_p = iota((2 * levels, LANES), 1)
    lane_l = iota((levels, LANES), 1)

    def piece(out_ref, in_ref, k, slot, s_sem, r_sem, target):
        return pltpu.make_async_remote_copy(
            src_ref=out_ref.at[k], dst_ref=in_ref.at[slot], send_sem=s_sem.at[k],
            recv_sem=r_sem.at[slot], device_id={"gx": target},
            device_id_type=pl.DeviceIdType.MESH)

    def each_piece(out_ref, in_ref, count, base, slots, s_sem, r_sem, start):
        for slot, cond in enumerate(slots):
            for k in range(count):
                target = base + k

                @pl.when(cond & (target != me))
                def _():
                    copy = piece(out_ref, in_ref, k, slot, s_sem, r_sem, target)
                    if start:
                        copy.start()
                    else:
                        copy.wait_send()

                if start:
                    @pl.when(cond & (target == me))
                    def _():
                        in_ref[slot] = out_ref[k]

    row_args = (row_out, row_in, tile_rows, row_base, (south, north), rs_sem, rr_sem)
    col_args = (col_out, col_in, COL_TILES, col_base, (west, east), cs_sem, cr_sem)

    @pl.when(south | north)
    def _():
        col_index = tj * tile_c + iota((levels, tile_c), 1)
        inverse = jnp.where(jnp.minimum(col_index, col_total - 1 - col_index) < ZONE, 0.5, 1.0)
        for w in range(ZONE):
            def pick(ref):
                return jnp.where(north, ref[:, tile_r - 1 - w, :], ref[:, w, :])
            weight = (1.0 - pick(omw)) * inverse
            first, last = two(weight * pick(z), weight * pick(z1))
            values = jnp.concatenate([first[:half], last[:half], first[half:], last[half:]], axis=0)
            for t in range(tile_rows):
                if cb % LANES == 0:
                    row_out[t, :, w * cb:(w + 1) * cb] = values[:, t * cb:(t + 1) * cb]
                    continue
                block, offset = divmod(w * cb, LANES)
                from_block, from_offset = divmod(t * cb, LANES)
                shift = (offset - from_offset) % LANES
                part = values[:, from_block * LANES:(from_block + 1) * LANES]
                part = pltpu.roll(part, shift, 1) if shift else part
                there = slice(block * LANES, (block + 1) * LANES)
                if offset:
                    part = jnp.where(lane_p >= offset, part, row_out[t, :, there])
                row_out[t, :, there] = part
        each_piece(*row_args, True)

    @pl.when(west | east)
    def _():
        for m, turned in enumerate(turned_columns(z1)):
            first, last = two(early[m], turned)
            strip[:, m, :] = first
            strip[:, half + m, :] = last
        lines = [jnp.where(east, strip[7 - w], strip[w]) for w in range(ZONE)]
        for k in range(COL_TILES):
            for f in range(2):
                value = jnp.zeros((levels, LANES), jnp.float32)
                for w in range(ZONE):
                    shift = (w * row_blk - f * tile_r - k * row_blk) % LANES
                    moved = pltpu.roll(lines[w], shift, 1) if shift else lines[w]
                    inside = (lane_l >= w * row_blk) & (lane_l < (w + 1) * row_blk)
                    value = jnp.where(inside, moved, value)
                col_out[k, f * levels:(f + 1) * levels, :] = value
        each_piece(*col_args, True)

    interior(z1, out)
    finish(out, 1)

    for slot in range(2):
        @pl.when(row_source[slot] != me)
        def _(slot=slot):
            piece(row_out, row_in, 0, slot, rs_sem, rr_sem, row_source[slot]).wait_recv()

        @pl.when(col_source[slot] != me)
        def _(slot=slot):
            piece(col_out, col_in, 0, slot, cs_sem, cr_sem, col_source[slot]).wait_recv()

    width = row_in.shape[2]
    side = ZONE * row_blk
    pts[:, :width] = row_in[0]
    pts[:, width:2 * width] = row_in[1]
    pts[:, 2 * width:] = jnp.where(lane_p < side, col_in[0], pltpu.roll(col_in[1], side, 1))

    for step in range(STEPS):
        for d in range(4):
            @pl.when(ways[d][0])
            def _(step=step, d=d):
                halo(step, d).wait_send()
    each_piece(*row_args, False)
    each_piece(*col_args, False)


def order_kernel(cb, width, adj, pts, slot_ref, adj_out, first_out, last_out, sem):
    levels, rim_blk = first_out.shape
    half = levels // 2
    span = ZONE * cb
    blocks = pts.shape[1] // LANES
    carry = pltpu.make_async_copy(adj, adj_out.at[0], sem)
    carry.start()
    for s in range(0, rim_blk, LANES):
        size = min(LANES, rim_blk - s)
        q = jnp.broadcast_to(slot_ref[s:s + size].reshape(1, size), (2 * levels, size))
        if size < LANES:
            q = jnp.concatenate([q, jnp.zeros((2 * levels, LANES - size), jnp.int32)], axis=1)
        place = jnp.where(q < span, q, jnp.where(q < 2 * span, q + (width - span),
                                                 q + 2 * (width - span)))
        high, low = place // LANES, place % LANES
        total = jnp.zeros((2 * levels, LANES), jnp.float32)
        for b in range(blocks):
            found = jnp.take_along_axis(pts[:, b * LANES:(b + 1) * LANES], low, axis=1)
            total = jnp.where(high == b, found, total)
        total = total[:, :size]
        first_out[:half, s:s + size] = total[:half]
        last_out[:half, s:s + size] = total[half:levels]
        first_out[half:, s:s + size] = total[levels:levels + half]
        last_out[half:, s:s + size] = total[levels + half:]
    carry.wait()


def body(adj_final, wind_east, wind_north, relax_weight, rim_slot):
    _, levels, tile_r, tile_c = adj_final.shape
    tile_count = lax.axis_size("gx")
    tile_rows = tile_count // COL_TILES
    cb = tile_c // tile_rows
    width = -(-ZONE * cb // LANES) * LANES
    f32 = jnp.float32
    field = pltpu.VMEM((levels, tile_r, tile_c), f32)
    dma = pltpu.SemaphoreType.DMA
    vmem, anywhere = pl.BlockSpec(memory_space=pltpu.VMEM), pl.BlockSpec(memory_space=pl.ANY)
    hbm = pl.BlockSpec(memory_space=pltpu.HBM)
    total = 2 * width + LANES
    adj, pts = pl.pallas_call(
        functools.partial(adjoint_kernel, tile_rows, cb),
        out_shape=(jax.ShapeDtypeStruct((levels, tile_r, tile_c), f32),
                   jax.ShapeDtypeStruct((2 * levels, total), f32)),
        in_specs=[hbm] * 4,
        out_specs=(vmem, vmem),
        scratch_shapes=[
            pltpu.SMEM(relax_weight.shape, f32),
            field, field, field, field, field,
            pltpu.VMEM((STEPS, 2, tile_r, LANES), f32),
            pltpu.VMEM((STEPS, 2, tile_r, LANES), f32),
            pltpu.VMEM((STEPS, 2, levels, tile_c), f32),
            pltpu.VMEM((STEPS, 2, levels, tile_c), f32),
            pltpu.VMEM((levels // 2, 8, LANES), f32),
            pltpu.VMEM((8, levels, LANES), f32),
            pltpu.VMEM((tile_rows, 2 * levels, width), f32),
            pltpu.VMEM((COL_TILES, 2 * levels, LANES), f32),
            pltpu.VMEM((2, 2 * levels, width), f32),
            pltpu.VMEM((2, 2 * levels, LANES), f32),
            dma, dma((3,)), dma((STEPS, 4)), dma((STEPS, 4)),
            dma((tile_rows,)), dma((2,)), dma((COL_TILES,)), dma((2,)),
        ],
        compiler_params=pltpu.CompilerParams(
            collective_id=0, has_side_effects=True, vmem_limit_bytes=32 * 1024 * 1024),
        cost_estimate=pl.CostEstimate(flops=10_000_000, bytes_accessed=2_200_000,
                                      transcendentals=0),
    )(*(pltpu.with_memory_space_constraint(x, pltpu.HBM)
        for x in (adj_final, wind_east, wind_north, relax_weight)))
    rim = jax.ShapeDtypeStruct((levels, rim_slot.shape[0]), f32)
    return pl.pallas_call(
        functools.partial(order_kernel, cb, width),
        out_shape=(jax.ShapeDtypeStruct((1, levels, tile_r, tile_c), f32), rim, rim),
        in_specs=[anywhere, vmem, vmem],
        out_specs=(hbm, vmem, vmem),
        scratch_shapes=[dma],
        compiler_params=pltpu.CompilerParams(vmem_limit_bytes=8 * 1024 * 1024),
    )(adj, pts, rim_slot)


def solution(mesh):
    return jax.shard_map(
        body,
        mesh=mesh,
        in_specs=(
            P("gx", "grp", None, None),
            P("gx", "grp", None, None),
            P("gx", "grp", None, None),
            P(),
            P("gx"),
        ),
        out_specs=(P("gx", "grp", None, None), P("grp", "gx"), P("grp", "gx")),
        check_vma=False,
    )
```
